768 devices in a mesh: row: 64 (over x, y, core), col: 12 (over z).
Axes of the slice: x: 4, y: 8, z: 12, core: 2. Of those that a mesh axis runs over, the one named last changes fastest.
Arguments:
- features: bfloat16 [196608, 128], P(('row', 'col')), may hold values from -6 to 6
- send_rows: int32 [64, 12, 2048], P('row', 'col'), may hold values from 0 to 255, as said below
- send_count: int32 [64, 12, 64], P('row', 'col'), may hold values from 1 to 32, as said below
- tile_values: bfloat16 [64, 12, 64, 128, 128], P('row', 'col'), may hold values from -0.375 to 0.375
- tile_dst: int32 [64, 12, 64], P('row', 'col'), may hold values from 0 to 23, as said below
- tile_src: int32 [64, 12, 64], P('row', 'col'), may hold values from 0 to 15
- tile_count: int32 [64, 12], P('row', 'col'), may hold values from 1 to 64, as said below
- labels: int32 [196608], P(('row', 'col')), may hold values from 0 to 171
- train_mask: int32 [196608], P(('row', 'col')), may hold values from 0 to 1
- w_self1: bfloat16 [128, 512], replicated, may hold values from -0.5 to 0.5
- w_neigh1: bfloat16 [128, 512], replicated, may hold values from -0.5 to 0.5
- w_self2: bfloat16 [512, 172], replicated, may hold values from -0.25 to 0.25
- w_neigh2: bfloat16 [512, 172], replicated, may hold values from -0.25 to 0.25
Outputs:
- grad_self1: float32 [128, 512], replicated
- grad_neigh1: float32 [128, 512], replicated
- grad_self2: float32 [512, 172], replicated
- grad_neigh2: float32 [512, 172], replicated
- loss: float32 [], replicated
The draws below stay inside these ranges and needn't reach their ends.
Inputs may be any that keep to these rules, and one draw needn't show every extreme that they name: `send_rows`: for each device and row peer the 32 entries name distinct local rows among the device's 256 nodes. `send_count`: some device sends exactly 32 live rows to some row peer. On each device the 64 tile slots have distinct pairs of tile_dst and tile_src. `tile_count`: some device has all 64 tiles live.
All inputs are finite; a program needn't handle non-finite values.
Results may differ from the reference program's by a relative error of at most 0.006.
The reference program's roundings to bfloat16 on the way count: a program that leaves them out, or rounds other values in their place, can miss the bound.
Values may be sent and summed in bfloat16 or wider, within the bound.
A program may use at most 64 MiB of HBM per device.

```python
import jax
import jax.numpy as jnp
from jax import lax

F = 128
H = 512
C = 172
V = 256
BLK = 128
CAP = 32
HALO = 2048
GROUP = 3072
TILES = 64
NODES = 196608
N_ROW = 64
N_COL = 12


def tile_layout(key):
    grid_cells = GROUP // BLK * (HALO // BLK)
    tile_keys = jax.random.split(key, N_ROW * N_COL)
    tile_order = jax.vmap(lambda single: jax.random.permutation(single, grid_cells))(tile_keys)[:, :TILES]
    return tile_order.reshape(N_ROW, N_COL, TILES).astype(jnp.int32)


def draw_tile_dst(key, part):
    tile_order = tile_layout(key)
    return (tile_order // (HALO // BLK)).astype(jnp.int32)


def draw_tile_src(key, part):
    tile_order = tile_layout(key)
    return (tile_order % (HALO // BLK)).astype(jnp.int32)


def draw_send_rows(key, part):
    key = jax.random.fold_in(key, 3)
    scores = jax.random.randint(key, (N_ROW, N_COL, N_ROW, V), 0, 2 ** 20) * V + jnp.arange(V, dtype=jnp.int32)
    chosen = jnp.argsort(scores, axis=-1, stable=True)[..., :CAP]
    return chosen.reshape(N_ROW, N_COL, HALO).astype(jnp.int32)


def draw_send_count(key, part):
    key = jax.random.fold_in(key, 5)
    first_key, second_key = jax.random.split(key)
    counts = jax.random.randint(first_key, (N_ROW * N_COL * N_ROW,), 1, CAP + 1)
    where_full = jax.random.randint(second_key, (), 0, N_ROW * N_COL * N_ROW)
    counts = counts.at[where_full].set(CAP)
    return counts.reshape(N_ROW, N_COL, N_ROW).astype(jnp.int32)


def draw_tile_count(key, part):
    key = jax.random.fold_in(key, 7)
    first_key, second_key = jax.random.split(key)
    uniform_int = jax.random.randint(first_key, (N_ROW * N_COL,), 1, 65)
    counts = (uniform_int * uniform_int * TILES + 4095) // 4096
    where_full = jax.random.randint(second_key, (), 0, N_ROW * N_COL)
    counts = counts.at[where_full].set(TILES)
    return counts.reshape(N_ROW, N_COL).astype(jnp.int32)


def draw_train_mask(key, part):
    key = jax.random.fold_in(key, 9)
    positions = jnp.arange(NODES, dtype=jnp.int32)
    uniform_int = jax.random.randint(key, (NODES,), 0, 5 * NODES)
    return (uniform_int < 2 * NODES + 3 * positions).astype(jnp.int32)


def set_ends(values, rng, smallest, high):
    longest = values.shape.index(max(values.shape))
    spots = []
    for shift in (0, 1):
        where = [jax.random.randint(jax.random.fold_in(rng, axis), (), 0, length) for axis, length in enumerate(values.shape)]
        where[longest] = (where[longest] + shift) % values.shape[longest]
        spots.append(tuple(where))
    return values.at[spots[0]].set(smallest).at[spots[1]].set(high)


def level_of(stream_key, shape, shards, least, high):
    loudness = 1.0
    for position, shards_of in shards:
        heights = jax.random.uniform(jax.random.fold_in(jax.random.fold_in(stream_key, 6), position), (shards_of,), jnp.float32, least / len(shards), high / len(shards))
        loudness = loudness * jnp.repeat(jnp.exp(heights), shape[position] // shards_of).reshape((-1,) + (1,) * (len(shape) - 1 - position))
    return loudness


def noise(rng, dims, width, bound, shards=(), held_as=jnp.bfloat16):
    array = width * jax.random.normal(rng, dims, jnp.float32)
    if shards:
        array = array * level_of(rng, dims, shards, -0.22, 0.18)
    return jnp.clip(array, -bound, bound).astype(held_as)


def setup_inputs(seed: int = 0) -> dict:
    key_list = jax.random.split(jax.random.key(seed), 14)
    features = noise(key_list[0], (NODES, F), 1.0, 6.0, ((0, 768),))
    send_rows = draw_send_rows(jax.random.fold_in(key_list[13], 71), 0)
    send_count = draw_send_count(jax.random.fold_in(key_list[13], 71), 0)
    tile_values = noise(key_list[3], (N_ROW, N_COL, TILES, BLK, BLK), (2 * BLK) ** -0.5, 0.375, ((0, 64), (1, 12)))
    tile_dst = draw_tile_dst(jax.random.fold_in(key_list[13], 71), 0)
    tile_src = draw_tile_src(jax.random.fold_in(key_list[13], 71), 0)
    tile_count = draw_tile_count(jax.random.fold_in(key_list[13], 71), 0)
    labels = set_ends(jax.random.randint(key_list[7], (NODES,), 0, C), jax.random.fold_in(key_list[7], 1), 0, C - 1).astype(jnp.int32)
    train_mask = draw_train_mask(jax.random.fold_in(key_list[13], 71), 0)
    w_self1 = noise(key_list[9], (F, H), F ** -0.5, 0.5)
    w_neigh1 = noise(key_list[10], (F, H), F ** -0.5, 0.5)
    w_self2 = noise(key_list[11], (H, C), H ** -0.5, 0.25)
    w_neigh2 = noise(key_list[12], (H, C), H ** -0.5, 0.25)
    return {"features": features, "send_rows": send_rows, "send_count": send_count, "tile_values": tile_values, "tile_dst": tile_dst, "tile_src": tile_src, "tile_count": tile_count, "labels": labels, "train_mask": train_mask, "w_self1": w_self1, "w_neigh1": w_neigh1, "w_self2": w_self2, "w_neigh2": w_neigh2}


full_precision = lax.Precision.HIGHEST

def tile_forward(halo_rows, tile_block, dest_block, source_block, live_count):
    row_width = halo_rows.shape[-1]
    source_rows = halo_rows.reshape(HALO // BLK, BLK, row_width)[source_block]
    products = jnp.einsum('tij,tjw->tiw', tile_block.astype(jnp.float32), source_rows.astype(jnp.float32), precision=full_precision)
    tile_live = (jnp.arange(TILES) < live_count).astype(jnp.float32)
    dest_place = (jnp.arange(GROUP // BLK)[:, None] == dest_block[None, :]).astype(jnp.float32) * tile_live[None, :]
    placed = jnp.einsum('dt,tiw->diw', dest_place, products, precision=full_precision)
    return placed.reshape(GROUP, row_width)

def tile_backward(group_grads, tile_block, dest_block, source_block, live_count):
    row_width = group_grads.shape[-1]
    dest_rows = group_grads.reshape(GROUP // BLK, BLK, row_width)[dest_block]
    products = jnp.einsum('tji,tjw->tiw', tile_block.astype(jnp.float32), dest_rows.astype(jnp.float32), precision=full_precision)
    tile_live = (jnp.arange(TILES) < live_count).astype(jnp.float32)
    source_place = (jnp.arange(HALO // BLK)[:, None] == source_block[None, :]).astype(jnp.float32) * tile_live[None, :]
    placed = jnp.einsum('st,tiw->siw', source_place, products, precision=full_precision)
    return placed.reshape(HALO, row_width).astype(jnp.bfloat16)

def aggregate_rows(node_rows, sent_index, sent_valid, tile_values, tile_dst, tile_src, tile_count):
    row_width = node_rows.shape[-1]
    node_grid = node_rows.reshape(N_ROW, N_COL, V, row_width)

    def one_group(group_index):
        chosen = sent_index[:, :, group_index, :]
        picked = jax.vmap(jax.vmap(lambda source, wanted: source[wanted]))(node_grid, chosen)
        picked = jnp.where(sent_valid[:, :, group_index, :, None], picked, jnp.zeros((), picked.dtype))
        halo_rows = jnp.transpose(picked, (1, 0, 2, 3)).reshape(N_COL, HALO, row_width)
        partial_sums = jax.vmap(tile_forward)(halo_rows, tile_values[group_index], tile_dst[group_index], tile_src[group_index], tile_count[group_index])
        return lax.optimization_barrier(jnp.sum(partial_sums, axis=0))
    grouped = lax.map(one_group, jnp.arange(N_ROW, dtype=jnp.int32))
    return grouped.reshape(N_ROW * GROUP, row_width).astype(jnp.bfloat16)

def spread_back(node_grads, sent_index, sent_valid, tile_values, tile_dst, tile_src, tile_count):
    row_width = node_grads.shape[-1]
    group_grid = node_grads.reshape(N_ROW, GROUP, row_width)
    row_ids = jnp.broadcast_to(jnp.arange(N_ROW, dtype=jnp.int32)[:, None, None], (N_ROW, N_COL, CAP))
    col_ids = jnp.broadcast_to(jnp.arange(N_COL, dtype=jnp.int32)[None, :, None], (N_ROW, N_COL, CAP))

    def add_group(group_index, summed_up):
        slot_grads = jax.vmap(tile_backward, in_axes=(None, 0, 0, 0, 0))(group_grid[group_index], tile_values[group_index], tile_dst[group_index], tile_src[group_index], tile_count[group_index])
        slot_grads = jnp.transpose(slot_grads.reshape(N_COL, N_ROW, CAP, row_width), (1, 0, 2, 3)).astype(jnp.float32)
        slot_grads = jnp.where(sent_valid[:, :, group_index, :, None], slot_grads, jnp.float32(0.0))
        return summed_up.at[row_ids, col_ids, sent_index[:, :, group_index, :]].add(slot_grads)
    summed_up = lax.fori_loop(0, N_ROW, add_group, jnp.zeros((N_ROW, N_COL, V, row_width), jnp.float32))
    return summed_up.reshape(NODES, row_width)

def reference(features, send_rows, send_count, tile_values, tile_dst, tile_src, tile_count, labels, train_mask, w_self1, w_neigh1, w_self2, w_neigh2):
    sent_index = send_rows.reshape(N_ROW, N_COL, N_ROW, CAP).astype(jnp.int32)
    sent_valid = jnp.arange(CAP)[None, None, None, :] < send_count[..., None]
    tiles = (tile_values, tile_dst, tile_src, tile_count)
    agg1 = aggregate_rows(features, sent_index, sent_valid, *tiles)
    pre1 = jnp.dot(features, w_self1, preferred_element_type=jnp.float32) + jnp.dot(agg1, w_neigh1, preferred_element_type=jnp.float32)
    hidden1 = jnp.maximum(pre1, 0.0).astype(jnp.bfloat16)
    neigh2 = jnp.dot(hidden1, w_neigh2, preferred_element_type=jnp.float32).astype(jnp.bfloat16)
    agg2 = aggregate_rows(neigh2, sent_index, sent_valid, *tiles)
    logits = jnp.dot(hidden1, w_self2, preferred_element_type=jnp.float32) + agg2.astype(jnp.float32)
    log_total = jnp.log(lax.optimization_barrier(jnp.sum(jnp.exp(logits), axis=-1)))
    label_hits = (jnp.arange(C)[None, :] == labels[:, None]).astype(jnp.float32)
    train_live = train_mask.astype(jnp.float32)
    cross = log_total - lax.optimization_barrier(jnp.sum(logits * label_hits, axis=-1))
    node_count = jnp.maximum(jnp.sum(train_live), 1.0)
    loss_sum = jnp.sum(train_live * cross)
    probability = jnp.exp(logits - log_total[:, None])
    grad_logits = (train_live[:, None] * (probability - label_hits)).astype(jnp.bfloat16)
    back_rows = spread_back(grad_logits, sent_index, sent_valid, *tiles).astype(jnp.bfloat16)
    grad_hidden = jnp.dot(grad_logits, w_self2.T, preferred_element_type=jnp.float32) + jnp.dot(back_rows, w_neigh2.T, preferred_element_type=jnp.float32)
    grad_pre1 = jnp.where(pre1 > 0, grad_hidden, 0.0).astype(jnp.bfloat16)
    grad_scale = 1.0 / jnp.sqrt(node_count)
    grad_self1 = jnp.dot(features.T, grad_pre1, preferred_element_type=jnp.float32) * grad_scale
    grad_neigh1 = jnp.dot(agg1.T, grad_pre1, preferred_element_type=jnp.float32) * grad_scale
    grad_self2 = jnp.dot(hidden1.T, grad_logits, preferred_element_type=jnp.float32) * grad_scale
    grad_neigh2 = jnp.dot(hidden1.T, back_rows, preferred_element_type=jnp.float32) * grad_scale
    return (grad_self1, grad_neigh1, grad_self2, grad_neigh2, loss_sum / node_count)
```

```python
import jax
import jax.numpy as jnp
from jax import lax
from jax.experimental import pallas as pl
from jax.experimental.pallas import tpu as pltpu
from jax.sharding import PartitionSpec as P

MESH = pl.DeviceIdType.MESH
f32, bf16, i32 = jnp.float32, jnp.bfloat16, jnp.int32

NX, NY = 4, 8
NR, NZ = 64, 12
CLASSES = 172
TAIL = CLASSES - 128
UP, DOWN = 6, 5


def mm(a, b):
    return jnp.dot(a, b, preferred_element_type=f32)


def mm_t(a, b):
    return lax.dot_general(a, b, (((0,), (0,)), ((), ())), preferred_element_type=f32)


def mm_nt(a, b):
    return lax.dot_general(a, b, (((1,), (1,)), ((), ())), preferred_element_type=f32)


def lanes_of(shape):
    return lax.broadcasted_iota(i32, shape, len(shape) - 1)


def split3(value):
    high = value.astype(bf16).astype(f32)
    middle = (value - high).astype(bf16).astype(f32)
    return high, middle, value - high - middle


def put_scalars(rows, loss, count):
    lanes = lanes_of(rows.shape)
    first = lax.broadcasted_iota(i32, rows.shape, len(rows.shape) - 2) == 0
    for at, part in enumerate(split3(loss) + split3(count)):
        rows = jnp.where(first & (lanes == TAIL + at), part.reshape((1,) * len(rows.shape)), rows)
    return rows


def get_scalars(rows):
    lanes = lanes_of(rows.shape)
    first = lax.broadcasted_iota(i32, rows.shape, 0) == 0

    def total(low):
        live = first & (lanes >= low) & (lanes < low + 3)
        picked = jnp.where(live, rows, 0.0)
        return jnp.sum(jnp.sum(picked, axis=1, keepdims=True), axis=0, keepdims=True)

    return total(TAIL), total(TAIL + 3)


def half_turn(rows):
    return pltpu.roll(rows, 64, axis=1)


def kernel(
    cell, feat, rows, cnt, tiles_hbm, lab, mask, ws1, wn1, w2,
    g1, g2, g3, g4, loss_out,
    tiles, dense, pick, s1, r1, s2, r2, s3, r3, wide,
    up_s, up_r, dn_s, dn_r, up2_s, up2_r, dn2_s, dn2_r, gbuf, st,
    pre1, hidden, agg1, gl, sl, neigh, back, mine, pair_r, hs, hr, zs, zr, fin,
    tile_sem, a1, a2, a3, us, ur, ds, dr, us2, ur2, ds2, dr2, gus, gur, gds, gdr,
    pair_sem, hsem, zsem, fsem, pair2_sem,
):
    me = lax.axis_index("row")
    z = lax.axis_index("col")
    core, chip = lax.rem(me, 2), me // 2
    x, y = chip // NY, lax.rem(chip, NY)
    above, below = lax.rem(z + 1, NZ), lax.rem(z + NZ - 1, NZ)
    partner = chip * 2 + 1 - core

    tile_copy = pltpu.make_async_copy(tiles_hbm, tiles.at[pl.ds(0, 64)], tile_sem)
    tile_copy.start()

    barrier = pltpu.get_barrier_semaphore()

    def greet_row(k, c):
        pl.semaphore_signal(barrier, inc=1, device_id=(lax.rem(me + k, NR), z), device_id_type=MESH)
        return c

    def greet_col(k, c):
        pl.semaphore_signal(barrier, inc=1, device_id=(me, lax.rem(z + k, NZ)), device_id_type=MESH)
        return c

    lax.fori_loop(1, NR, greet_row, 0)
    lax.fori_loop(1, NZ, greet_col, 0)

    peer_of = lax.broadcasted_iota(i32, (NR, 2048), 1) // 32 == lax.broadcasted_iota(i32, (NR, 2048), 0)
    counts = jnp.broadcast_to(cnt[...].astype(f32), (8, NR)).astype(bf16)
    live_rows = mm(counts, peer_of.astype(f32).astype(bf16))[0:1]
    place = lax.rem(lax.broadcasted_iota(i32, (1, 2048), 1), 32).astype(f32)
    wanted = jnp.where(place < live_rows, rows[...].astype(f32), -1.0)
    tall = jnp.transpose(jnp.broadcast_to(wanted, (128, 2048)))
    node = lax.broadcasted_iota(i32, (2048, 128), 1).astype(f32)
    pick[:, 0:128] = (tall == node).astype(f32).astype(bf16)
    pick[:, 128:256] = (tall == node + 128.0).astype(f32).astype(bf16)

    pl.semaphore_wait(barrier, NR - 1 + NZ - 1)

    def group_of(dx):
        return lax.rem(x + dx, NX)

    def send_group(dx, src, dst, sem):
        def one(i, c):
            py = lax.rem(y + lax.rem(i // 2 * 3, NY), NY)
            peer = (group_of(dx) * NY + py) * 2 + lax.rem(core + lax.rem(i, 2), 2)
            pltpu.make_async_remote_copy(
                src_ref=src.at[peer], dst_ref=dst.at[me], send_sem=sem.at[0], recv_sem=sem.at[1],
                device_id=(peer, z), device_id_type=MESH,
            ).start()
            return c

        lax.fori_loop(1 if dx == 0 else 0, 16, one, 0)

    def all_of(src, dst, sem, number):
        return pltpu.make_async_remote_copy(
            src_ref=src.at[pl.ds(0, number)], dst_ref=dst.at[pl.ds(0, number)],
            send_sem=sem.at[0], recv_sem=sem.at[1], device_id=(partner, z), device_id_type=MESH,
        )

    def pack_group(dx, value, dst, scalars):
        first = group_of(dx) * 16
        dst[pl.ds(first, 16), 0:32, :] = value[:, 0:128].astype(bf16).reshape(16, 32, 128)
        tail = value[:, 128:256].reshape(16, 2, 16, 128)
        low, high = tail[:, 0], tail[:, 1]
        high = half_turn(high.reshape(256, 128)).reshape(16, 16, 128)
        both = low + high
        if scalars is not None:
            both = put_scalars(both, *scalars)
        dst[pl.ds(first, 16), 32:48, :] = both.astype(bf16)

    def unpack_rows(src):
        def one(i, c):
            part = pl.ds(i * 8, 8)
            wide[part, :, 0:128] = src[part, 0:32, :]
            tail = src[part, 32:48, :].astype(f32).reshape(128, 128)
            live = lanes_of((128, 128)) < TAIL
            low = jnp.where(live, tail, 0.0).astype(bf16)
            high = jnp.where(live, half_turn(tail), 0.0).astype(bf16)
            wide[part, 0:16, 128:256] = low.reshape(8, 16, 128)
            wide[part, 16:32, 128:256] = high.reshape(8, 16, 128)
            return c

        lax.fori_loop(0, 8, one, 0)

    order = (2, 1, 3, 0)
    for dx in order:
        at = pl.ds(pl.multiple_of(group_of(dx) * 512, 512), 512)
        block = mm(pick[at, :], feat[...]).astype(bf16)
        s1[pl.ds(group_of(dx) * 16, 16)] = block.reshape(16, 32, 128)
        send_group(dx, s1, r1, a1)
    r1[me] = s1[me]

    tile_copy.wait()
    tiles[64] = jnp.zeros((128, 128), bf16)

    def lay(d, c):
        for s in range(16):
            at = pl.ds(pl.multiple_of(d * 128, 128), 128)
            dense[at, s * 128 : (s + 1) * 128] = tiles[cell[d * 16 + s]]
        return c

    lax.fori_loop(0, 24, lay, 0)
    pre1[...] = mm(feat[...], ws1[...])
    up_r[0] = jnp.zeros(up_r.shape[1:], f32)
    dn_r[0] = jnp.zeros(dn_r.shape[1:], f32)
    up2_r[0] = jnp.zeros(up2_r.shape[1:], bf16)
    dn2_r[0] = jnp.zeros(dn2_r.shape[1:], bf16)

    def hop(src, dst, ssem, rsem, j, h, to):
        half = src.shape[1] // 2
        part = pl.ds(h * half, half)
        return pltpu.make_async_remote_copy(
            src_ref=src.at[j, part], dst_ref=dst.at[j + 1, part],
            send_sem=ssem.at[j, h], recv_sem=rsem.at[j, h], device_id=(me, to), device_id_type=MESH,
        )

    def ring_sum(chunk, ups, upr, dns, dnr, uss, urs, dss, drs):
        half = ups.shape[1] // 2

        def move(value, src, dst, ssem, rsem, j, to):
            for h in range(2):
                part = pl.ds(h * half, half)

                @pl.when(j > 0)
                def _():
                    hop(src, dst, ssem, rsem, j - 1, h, to).wait_recv()

                got = dst[j, part].astype(f32)
                src[j, part] = (value[h * half : (h + 1) * half] + got).astype(src.dtype)
                hop(src, dst, ssem, rsem, j, h, to).start()

        def step(j, c):
            high = chunk(lax.rem(z + UP - j, NZ))
            low = chunk(lax.rem(z + NZ - DOWN + j, NZ))
            move(high, ups, upr, uss, urs, j, above)
            move(low, dns, dnr, dss, drs, j, below)
            return c

        lax.fori_loop(0, DOWN, step, 0)
        move(chunk(above), ups, upr, uss, urs, UP - 1, above)
        own = chunk(z)
        for h in range(2):
            hop(dns, dnr, dss, drs, DOWN - 1, h, below).wait_recv()
        for h in range(2):
            hop(ups, upr, uss, urs, UP - 1, h, above).wait_recv()
        return own + dnr[DOWN].astype(f32) + upr[UP].astype(f32)

    def ring_sent(ups, upr, dns, dnr, uss, urs, dss, drs):
        def sent(j, c):
            for h in range(2):
                hop(ups, upr, uss, urs, j, h, above).wait_send()

                @pl.when(j < DOWN)
                def _():
                    hop(dns, dnr, dss, drs, j, h, below).wait_send()

            return c

        lax.fori_loop(0, UP, sent, 0)

    def block_rows(o):
        return dense[pl.ds(pl.multiple_of(o * 256, 256), 256), :]

    all_of(s1, r1, a1, NR - 1).wait_recv()

    def chunk1(o):
        return mm(block_rows(o), r1[...].reshape(2048, 128))

    ring1 = (up_s, up_r, dn_s, dn_r, us, ur, ds, dr)
    agg1[...] = ring_sum(chunk1, *ring1).astype(bf16)

    pre = pre1[...] + mm(agg1[...], wn1[...])
    pre1[...] = pre
    hidden[...] = jnp.maximum(pre, 0.0).astype(bf16)
    neigh[...] = mm(hidden[...], w2[:, 256:512]).astype(bf16)

    for dx in order:
        at = pl.ds(pl.multiple_of(group_of(dx) * 512, 512), 512)
        pack_group(dx, mm(pick[at, :], neigh[...]), s2, None)
        send_group(dx, s2, r2, a2)
    r2[me] = s2[me]
    sl[...] = mm(hidden[...], w2[:, 0:256])
    ring_sent(*ring1)
    all_of(s1, r1, a1, NR - 1).wait_send()
    all_of(s2, r2, a2, NR - 1).wait_recv()
    unpack_rows(r2)

    def pack_chunk(full):
        tail = full[:, 128:256]
        both = tail[0:128] + half_turn(tail[128:256])
        return jnp.concatenate([full[:, 0:128], both], axis=0)

    def unpack_chunk(packed):
        tail = packed[256:384]
        live = lanes_of((128, 128)) < TAIL
        low = jnp.where(live, tail, 0.0)
        high = jnp.where(live, half_turn(tail), 0.0)
        return jnp.concatenate([packed[0:256], jnp.concatenate([low, high], axis=0)], axis=1)

    def chunk2(o):
        return pack_chunk(mm(block_rows(o), wide[...].reshape(2048, 256)))

    ring2 = (up2_s, up2_r, dn2_s, dn2_r, us2, ur2, ds2, dr2)
    agg2 = unpack_chunk(ring_sum(chunk2, *ring2)).astype(bf16).astype(f32)

    logits = sl[...] + agg2
    lanes = lanes_of((256, 256))
    live = lanes < CLASSES

    def tall_of(ref):
        one = jnp.transpose(jnp.broadcast_to(ref[...].astype(f32), (128, 256)))
        return jnp.concatenate([one, one], axis=1)

    hit = lanes.astype(f32) == tall_of(lab)
    train = tall_of(mask)
    log_total = jnp.log(jnp.sum(jnp.where(live, jnp.exp(logits), 0.0), axis=1, keepdims=True))
    cross = log_total - jnp.sum(jnp.where(hit, logits, 0.0), axis=1, keepdims=True)
    prob = jnp.where(live, jnp.exp(logits - log_total), 0.0)
    grad = (train * (prob - hit.astype(f32))).astype(bf16)
    gl[...] = grad
    loss_part = jnp.sum(train[:, 0:1] * cross, axis=0, keepdims=True)
    count_part = jnp.sum(train[:, 0:1], axis=0, keepdims=True)

    packed = pack_chunk(grad.astype(f32))
    gbuf[z, 0:256] = packed[0:256].astype(bf16)
    gbuf[z, 256:384] = put_scalars(packed[256:384], loss_part, count_part).astype(bf16)

    def pass_on(owner, ssem, rsem, j, h, to):
        part = pl.ds(h * 192, 192)
        return pltpu.make_async_remote_copy(
            src_ref=gbuf.at[owner, part], dst_ref=gbuf.at[owner, part],
            send_sem=ssem.at[j, h], recv_sem=rsem.at[j, h], device_id=(me, to), device_id_type=MESH,
        )

    def up_hop(j, h):
        return pass_on(lax.rem(z + NZ - j, NZ), gus, gur, j, h, above)

    def down_hop(j, h):
        return pass_on(lax.rem(z + j, NZ), gds, gdr, j, h, below)

    def back_chunk(o):
        full = unpack_chunk(gbuf[o].astype(f32))
        return mm(jnp.transpose(full).astype(bf16), block_rows(o))

    for h in range(2):
        up_hop(0, h).start()
        down_hop(0, h).start()
    st[...] = back_chunk(z)

    def gather_step(j, c):
        for h in range(2):
            up_hop(j - 1, h).wait_recv()
            up_hop(j, h).start()
            down_hop(j - 1, h).wait_recv()

            @pl.when(j < DOWN)
            def _():
                down_hop(j, h).start()

        st[...] += back_chunk(lax.rem(z + NZ - j, NZ)) + back_chunk(lax.rem(z + j, NZ))
        return c

    lax.fori_loop(1, UP, gather_step, 0)
    for h in range(2):
        up_hop(UP - 1, h).wait_recv()
    st[...] += back_chunk(lax.rem(z + NZ - UP, NZ))
    col_sums = get_scalars(jnp.sum(gbuf[:, 256:272, :].astype(f32), axis=0))

    for dx in order:
        at = pl.ds(pl.multiple_of(group_of(dx) * 512, 512), 512)
        pack_group(dx, jnp.transpose(st[:, at]), s3, col_sums)
        send_group(dx, s3, r3, a3)
    r3[me] = s3[me]

    ring_sent(*ring2)

    def gather_sent(j, c):
        for h in range(2):
            up_hop(j, h).wait_send()

            @pl.when(j < DOWN)
            def _():
                down_hop(j, h).wait_send()

        return c

    lax.fori_loop(0, UP, gather_sent, 0)
    all_of(s2, r2, a2, NR - 1).wait_send()
    all_of(s3, r3, a3, NR - 1).wait_recv()
    unpack_rows(r3)
    loss_sum, node_count = get_scalars(jnp.sum(r3[:, 32:48, :].astype(f32), axis=0))

    back[...] = mm_t(pick[...], wide[...].reshape(2048, 256)).astype(bf16)

    grad_hidden = mm_nt(gl[...], w2[:, 0:256]) + mm_nt(back[...], w2[:, 256:512])
    grad_pre = jnp.where(pre1[...] > 0, grad_hidden, 0.0).astype(bf16)
    parts = (
        mm_t(feat[...], grad_pre),
        mm_t(agg1[...], grad_pre),
        mm_t(gl[...], hidden[...])[0:192],
        mm_t(back[...], hidden[...])[0:192],
        jnp.zeros((128, 512), f32),
    )
    for b in range(4):
        cut = jnp.concatenate([part[:, b * 128 : (b + 1) * 128] for part in parts], axis=0)
        mine[b * 16 : (b + 1) * 16] = cut.reshape(16, 48, 128)

    def to_pair(src, dst, sem, first_s, first_d):
        return pltpu.make_async_remote_copy(
            src_ref=src.at[pl.ds(first_s, 32)], dst_ref=dst.at[pl.ds(first_d, 32)],
            send_sem=sem.at[0], recv_sem=sem.at[1], device_id=(partner, z), device_id_type=MESH,
        )

    swap = to_pair(mine, pair_r, pair_sem, (1 - core) * 32, 0)
    swap.start()
    swap.wait_recv()
    hs[...] = (mine[pl.ds(core * 32, 32)] + pair_r[...]).astype(bf16)

    def plane_send(k, src, dst, at, sem):
        other = lax.rem(x + k // NY, NX) * NY + lax.rem(y + lax.rem(k * 3, NY), NY)
        source = src.at[other] if at is None else src.at[at]
        target = dst.at[chip] if at is None else dst.at[at]
        pltpu.make_async_remote_copy(
            src_ref=source, dst_ref=target, send_sem=sem.at[0], recv_sem=sem.at[1],
            device_id=(other * 2 + core, z), device_id_type=MESH,
        ).start()

    def scatter_one(k, c):
        plane_send(k, hs, hr, None, hsem)
        return c

    lax.fori_loop(1, 32, scatter_one, 0)
    hr[chip] = hs[chip]
    all_of(s3, r3, a3, NR - 1).wait_send()
    swap.wait_send()
    all_of(hs, hr, hsem, 31).wait_recv()
    zs[...] = jnp.sum(hr[...].astype(f32), axis=0).astype(bf16)

    def planes_one(k, c):
        pltpu.make_async_remote_copy(
            src_ref=zs, dst_ref=zr.at[z], send_sem=zsem.at[0], recv_sem=zsem.at[1],
            device_id=(me, lax.rem(z + k, NZ)), device_id_type=MESH,
        ).start()
        return c

    lax.fori_loop(1, NZ, planes_one, 0)
    zr[z] = zs[...]
    all_of(hs, hr, hsem, 31).wait_send()
    all_of(zr, zr, zsem, NZ - 1).wait_recv()
    piece = core * 32 + chip
    fin[piece] = jnp.sum(zr[...].astype(f32), axis=0).astype(bf16)

    def gather_one(k, c):
        plane_send(k, fin, fin, piece, fsem)
        return c

    lax.fori_loop(1, 32, gather_one, 0)
    all_of(zr, zr, zsem, NZ - 1).wait_send()
    all_of(fin, fin, fsem, 31).wait_recv()
    swap2 = to_pair(fin, fin, pair2_sem, core * 32, core * 32)
    swap2.start()

    node_count = jnp.maximum(node_count, 1.0)
    scale = 1.0 / jnp.sqrt(node_count)
    loss_out[...] = jnp.broadcast_to(loss_sum / node_count, (8, 128))
    swap2.wait_recv()
    for b in range(4):
        at = slice(b * 128, (b + 1) * 128)
        cut = fin[b * 16 : (b + 1) * 16].astype(f32).reshape(768, 128) * scale
        g1[:, at] = cut[0:128]
        g2[:, at] = cut[128:256]
        g3[at, :] = jnp.transpose(cut[256:512])[:, 0:CLASSES]
        g4[at, :] = jnp.transpose(cut[448:704])[:, 0:CLASSES]
    all_of(fin, fin, fsem, 31).wait_send()
    swap2.wait_send()


def shards(
    features, send_rows, send_count, tile_values, tile_dst, tile_src, tile_count,
    labels, train_mask, w_self1, w_neigh1, w_self2, w_neigh2,
):
    slots = jnp.arange(64, dtype=i32)
    where = tile_dst.reshape(1, 64) * 16 + tile_src.reshape(1, 64)
    lives = (jnp.arange(384, dtype=i32)[:, None] == where) & (slots < tile_count.reshape(()))[None, :]
    cell = jnp.min(jnp.where(lives, slots[None, :], 64), axis=1)
    fill = ((0, 0), (0, 256 - CLASSES))
    w2 = jnp.concatenate([jnp.pad(w_self2, fill), jnp.pad(w_neigh2, fill)], axis=1)
    vm = pl.BlockSpec(memory_space=pltpu.VMEM)
    sm = pl.BlockSpec(memory_space=pltpu.SMEM)
    V = pltpu.VMEM
    dma = pltpu.SemaphoreType.DMA
    out = pl.pallas_call(
        kernel,
        out_shape=[
            jax.ShapeDtypeStruct((128, 512), f32),
            jax.ShapeDtypeStruct((128, 512), f32),
            jax.ShapeDtypeStruct((512, CLASSES), f32),
            jax.ShapeDtypeStruct((512, CLASSES), f32),
            jax.ShapeDtypeStruct((8, 128), f32),
        ],
        in_specs=[sm, vm, vm, vm, pl.BlockSpec(memory_space=pl.ANY), vm, vm, vm, vm, vm],
        out_specs=[vm] * 5,
        scratch_shapes=[
            V((65, 128, 128), bf16),
            V((3072, 2048), bf16),
            V((2048, 256), bf16),
            V((64, 32, 128), bf16), V((64, 32, 128), bf16),
            V((64, 48, 128), bf16), V((64, 48, 128), bf16),
            V((64, 48, 128), bf16), V((64, 48, 128), bf16),
            V((64, 32, 256), bf16),
            V((UP, 256, 128), f32), V((UP + 1, 256, 128), f32),
            V((DOWN, 256, 128), f32), V((DOWN + 1, 256, 128), f32),
            V((UP, 384, 128), bf16), V((UP + 1, 384, 128), bf16),
            V((DOWN, 384, 128), bf16), V((DOWN + 1, 384, 128), bf16),
            V((NZ, 384, 128), bf16),
            V((256, 2048), f32),
            V((256, 512), f32),
            V((256, 512), bf16),
            V((256, 128), bf16),
            V((256, 256), bf16),
            V((256, 256), f32),
            V((256, 256), bf16),
            V((256, 256), bf16),
            V((64, 48, 128), f32), V((32, 48, 128), f32),
            V((32, 48, 128), bf16), V((32, 48, 128), bf16),
            V((48, 128), bf16), V((NZ, 48, 128), bf16),
            V((64, 48, 128), bf16),
            dma, dma((2,)), dma((2,)), dma((2,)),
            dma((UP, 2)), dma((UP, 2)), dma((DOWN, 2)), dma((DOWN, 2)),
            dma((UP, 2)), dma((UP, 2)), dma((DOWN, 2)), dma((DOWN, 2)),
            dma((UP, 2)), dma((UP, 2)), dma((DOWN, 2)), dma((DOWN, 2)),
            dma((2,)), dma((2,)), dma((2,)), dma((2,)), dma((2,)),
        ],
        compiler_params=pltpu.CompilerParams(
            collective_id=0, has_side_effects=True, vmem_limit_bytes=56 * 1024 * 1024
        ),
        name="sage_step",
    )(
        cell, features, send_rows.reshape(1, 2048), send_count.reshape(1, 64),
        tile_values.reshape(64, 128, 128), labels.reshape(1, 256), train_mask.reshape(1, 256),
        w_self1, w_neigh1, w2,
    )
    return (*out[:4], out[4][0, 0])


def solution(mesh):
    in_specs = (
        P(("row", "col"), None),
        P("row", "col", None),
        P("row", "col", None),
        P("row", "col", None, None, None),
        P("row", "col", None),
        P("row", "col", None),
        P("row", "col"),
        P(("row", "col")),
        P(("row", "col")),
        P(),
        P(),
        P(),
        P(),
    )
    out_specs = (P(), P(), P(), P(), P())
    return jax.shard_map(shards, mesh=mesh, in_specs=in_specs, out_specs=out_specs, check_vma=False)
```

```python
import jax
import jax.numpy as jnp
from jax import lax
from jax.experimental import pallas as pl
from jax.experimental.pallas import tpu as pltpu
from jax.sharding import PartitionSpec as P

MESH = pl.DeviceIdType.MESH
f32, bf16, i32 = jnp.float32, jnp.bfloat16, jnp.int32

NX, NY = 4, 8
NR, NZ = 64, 12
CLASSES = 172
PARTS = 4
TAIL = CLASSES - 128
UP, DOWN = 6, 5


def mm(a, b):
    return jnp.dot(a, b, preferred_element_type=f32)


def mm_t(a, b):
    return lax.dot_general(a, b, (((0,), (0,)), ((), ())), preferred_element_type=f32)


def mm_nt(a, b):
    return lax.dot_general(a, b, (((1,), (1,)), ((), ())), preferred_element_type=f32)


def lanes_of(shape):
    return lax.broadcasted_iota(i32, shape, len(shape) - 1)


def split3(value):
    high = value.astype(bf16).astype(f32)
    middle = (value - high).astype(bf16).astype(f32)
    return high, middle, value - high - middle


def put_scalars(rows, loss, count):
    lanes = lanes_of(rows.shape)
    first = lax.broadcasted_iota(i32, rows.shape, len(rows.shape) - 2) == 0
    for at, part in enumerate(split3(loss) + split3(count)):
        rows = jnp.where(first & (lanes == TAIL + at), part.reshape((1,) * len(rows.shape)), rows)
    return rows


def get_scalars(rows):
    lanes = lanes_of(rows.shape)
    first = lax.broadcasted_iota(i32, rows.shape, 0) == 0

    def total(low):
        live = first & (lanes >= low) & (lanes < low + 3)
        picked = jnp.where(live, rows, 0.0)
        return jnp.sum(jnp.sum(picked, axis=1, keepdims=True), axis=0, keepdims=True)

    return total(TAIL), total(TAIL + 3)


def half_turn(rows):
    return pltpu.roll(rows, 64, axis=1)


def kernel(
    cell, feat, rows, cnt, tiles_hbm, lab, mask, ws1, wn1, ws2t, wn2t,
    fin_out, fin_e_out, sums_out,
    w2t, tiles, dense, pick, s1, r1, s2, r2, s3, r3, wide,
    up_s, up_r, dn_s, dn_r, up2_s, up2_r, dn2_s, dn2_r, gbuf, st, own1, own2,
    pre1, hidden, agg1, gl, sl, neigh, back, mine, pair_r, hs, hr, zs, zr, fin,
    mine_e, pair_e, hs_e, hr_e, zs_e, zr_e, fin_e,
    tile_sem, a1, a2, a3, us, ur, ds, dr, us2, ur2, ds2, dr2, gus, gur, gds, gdr,
    pair_sem, hsem, zsem, fsem, pair2_sem, pair_e_sem, h_e_sem, z_e_sem, f_e_sem, pair2_e_sem,
):
    me = lax.axis_index("row")
    z = lax.axis_index("col")
    core, chip = lax.rem(me, 2), me // 2
    x, y = chip // NY, lax.rem(chip, NY)
    above, below = lax.rem(z + 1, NZ), lax.rem(z + NZ - 1, NZ)
    partner = chip * 2 + 1 - core

    tile_copy = pltpu.make_async_copy(tiles_hbm, tiles.at[pl.ds(0, 64)], tile_sem)
    tile_copy.start()

    barrier = pltpu.get_barrier_semaphore()

    def greet_row(k, c):
        pl.semaphore_signal(barrier, inc=1, device_id=(lax.rem(me + k, NR), z), device_id_type=MESH)
        return c

    def greet_col(k, c):
        pl.semaphore_signal(barrier, inc=1, device_id=(me, lax.rem(z + k, NZ)), device_id_type=MESH)
        return c

    lax.fori_loop(1, NR, greet_row, 0)
    lax.fori_loop(1, NZ, greet_col, 0)

    peer_of = lax.broadcasted_iota(i32, (NR, 2048), 1) // 32 == lax.broadcasted_iota(i32, (NR, 2048), 0)
    counts = jnp.broadcast_to(cnt[...].astype(f32), (8, NR)).astype(bf16)
    live_rows = mm(counts, peer_of.astype(f32).astype(bf16))[0:1]
    place = lax.rem(lax.broadcasted_iota(i32, (1, 2048), 1), 32).astype(f32)
    wanted = jnp.where(place < live_rows, rows[...].astype(f32), -1.0)
    tall = jnp.transpose(jnp.broadcast_to(wanted, (128, 2048)))
    node = lax.broadcasted_iota(i32, (2048, 128), 1).astype(f32)
    pick[:, 0:128] = (tall == node).astype(f32).astype(bf16)
    pick[:, 128:256] = (tall == node + 128.0).astype(f32).astype(bf16)

    pl.semaphore_wait(barrier, NR - 1 + NZ - 1)

    def group_of(dx):
        return lax.rem(x + dx, NX)

    def send_group(dx, src, dst, sem):
        def one(i, c):
            py = lax.rem(y + lax.rem(i // 2 * 3, NY), NY)
            peer = (group_of(dx) * NY + py) * 2 + lax.rem(core + lax.rem(i, 2), 2)
            pltpu.make_async_remote_copy(
                src_ref=src.at[peer], dst_ref=dst.at[me], send_sem=sem.at[0], recv_sem=sem.at[1 + dx],
                device_id=(peer, z), device_id_type=MESH,
            ).start()
            return c

        lax.fori_loop(1 if dx == 0 else 0, 16, one, 0)

    def from_group(dx):
        return lax.rem(x + NX - dx, NX)

    def wait_group(dx, src, dst, sem):
        number = 15 if dx == 0 else 16
        pltpu.make_async_remote_copy(
            src_ref=src.at[pl.ds(0, number)], dst_ref=dst.at[pl.ds(0, number)],
            send_sem=sem.at[0], recv_sem=sem.at[1 + dx], device_id=(partner, z), device_id_type=MESH,
        ).wait_recv()

    def all_of(src, dst, sem, number):
        return pltpu.make_async_remote_copy(
            src_ref=src.at[pl.ds(0, number)], dst_ref=dst.at[pl.ds(0, number)],
            send_sem=sem.at[0], recv_sem=sem.at[1], device_id=(partner, z), device_id_type=MESH,
        )

    def pack_group(dx, value, dst, scalars):
        first = group_of(dx) * 16
        dst[pl.ds(first, 16), 0:32, :] = value[:, 0:128].astype(bf16).reshape(16, 32, 128)
        tail = value[:, 128:256].reshape(16, 2, 16, 128)
        low, high = tail[:, 0], tail[:, 1]
        high = half_turn(high.reshape(256, 128)).reshape(16, 16, 128)
        both = low + high
        if scalars is not None:
            both = put_scalars(both, *scalars)
        dst[pl.ds(first, 16), 32:48, :] = both.astype(bf16)

    def unpack_group(dx, src):
        def one(i, c):
            part = pl.ds(from_group(dx) * 16 + i * 8, 8)
            wide[part, :, 0:128] = src[part, 0:32, :]
            tail = src[part, 32:48, :].astype(f32).reshape(128, 128)
            live = lanes_of((128, 128)) < TAIL
            low = jnp.where(live, tail, 0.0).astype(bf16)
            high = jnp.where(live, half_turn(tail), 0.0).astype(bf16)
            wide[part, 0:16, 128:256] = low.reshape(8, 16, 128)
            wide[part, 16:32, 128:256] = high.reshape(8, 16, 128)
            return c

        lax.fori_loop(0, 2, one, 0)

    order = (2, 1, 3, 0)
    for dx in order:
        at = pl.ds(pl.multiple_of(group_of(dx) * 512, 512), 512)
        block = mm(pick[at, :], feat[...]).astype(bf16)
        s1[pl.ds(group_of(dx) * 16, 16)] = block.reshape(16, 32, 128)
        send_group(dx, s1, r1, a1)
    r1[me] = s1[me]

    w2t[...] = jnp.zeros(w2t.shape, bf16)
    w2t[0:CLASSES] = ws2t[...]
    w2t[256 : 256 + CLASSES] = wn2t[...]

    tile_copy.wait()
    tiles[64] = jnp.zeros((128, 128), bf16)

    def lay(d, c):
        for s in range(16):
            at = pl.ds(pl.multiple_of(d * 128, 128), 128)
            dense[at, s * 128 : (s + 1) * 128] = tiles[cell[d * 16 + s]]
        return c

    lax.fori_loop(0, 24, lay, 0)
    pre1[...] = mm(feat[...], ws1[...])
    up_r[0] = jnp.zeros(up_r.shape[1:], f32)
    dn_r[0] = jnp.zeros(dn_r.shape[1:], f32)
    up2_r[0] = jnp.zeros(up2_r.shape[1:], bf16)
    dn2_r[0] = jnp.zeros(dn2_r.shape[1:], bf16)

    def hop(src, dst, ssem, rsem, j, h, to):
        size = src.shape[1] // PARTS
        part = pl.ds(h * size, size)
        return pltpu.make_async_remote_copy(
            src_ref=src.at[j, part], dst_ref=dst.at[j + 1, part],
            send_sem=ssem.at[j, h], recv_sem=rsem.at[j, h], device_id=(me, to), device_id_type=MESH,
        )

    def ring_sum(chunk, own_part, ups, upr, dns, dnr, uss, urs, dss, drs):
        size = ups.shape[1] // PARTS

        def move(way, h, src, dst, ssem, rsem, j, to):
            part = pl.ds(h * size, size)

            @pl.when(j > 0)
            def _():
                hop(src, dst, ssem, rsem, j - 1, h, to).wait_recv()

            mine_now = own_part[lax.rem(j, 2), way, part]
            src[j, part] = (mine_now + dst[j, part].astype(f32)).astype(src.dtype)
            hop(src, dst, ssem, rsem, j, h, to).start()

        def compute(j):
            own_part[lax.rem(j, 2), 0] = chunk(lax.rem(z + UP - j, NZ))
            own_part[lax.rem(j, 2), 1] = chunk(lax.rem(z + NZ - DOWN + j, NZ))

        def step(j, c):
            for h in range(PARTS):
                if h == PARTS // 2:
                    compute(j + 1)
                move(0, h, ups, upr, uss, urs, j, above)
                move(1, h, dns, dnr, dss, drs, j, below)
            return c

        compute(jnp.int32(0))
        lax.fori_loop(0, DOWN, step, 0)
        last = jnp.int32(DOWN)
        for h in range(PARTS):
            move(0, h, ups, upr, uss, urs, last, above)
        for h in range(PARTS):
            hop(dns, dnr, dss, drs, DOWN - 1, h, below).wait_recv()
        for h in range(PARTS):
            hop(ups, upr, uss, urs, UP - 1, h, above).wait_recv()
        return own_part[DOWN % 2, 1] + dnr[DOWN].astype(f32) + upr[UP].astype(f32)

    def ring_sent(ups, upr, dns, dnr, uss, urs, dss, drs):
        def sent(j, c):
            for h in range(PARTS):
                hop(ups, upr, uss, urs, j, h, above).wait_send()

                @pl.when(j < DOWN)
                def _():
                    hop(dns, dnr, dss, drs, j, h, below).wait_send()

            return c

        lax.fori_loop(0, UP, sent, 0)

    def block_rows(o):
        return dense[pl.ds(pl.multiple_of(o * 256, 256), 256), :]

    for dx in order:
        wait_group(dx, s1, r1, a1)

    def chunk1(o):
        return mm(block_rows(o), r1[...].reshape(2048, 128))

    ring1 = (up_s, up_r, dn_s, dn_r, us, ur, ds, dr)
    agg1[...] = ring_sum(chunk1, own1, *ring1).astype(bf16)

    pre = pre1[...] + mm(agg1[...], wn1[...])
    pre1[...] = pre
    hidden[...] = jnp.maximum(pre, 0.0).astype(bf16)
    neigh[...] = mm_nt(hidden[...], w2t[256:512]).astype(bf16)

    for dx in order:
        at = pl.ds(pl.multiple_of(group_of(dx) * 512, 512), 512)
        pack_group(dx, mm(pick[at, :], neigh[...]), s2, None)
        send_group(dx, s2, r2, a2)
    r2[me] = s2[me]
    sl[...] = mm_nt(hidden[...], w2t[0:256])
    ring_sent(*ring1)
    all_of(s1, r1, a1, NR - 1).wait_send()
    for dx in order:
        wait_group(dx, s2, r2, a2)
        unpack_group(dx, r2)

    def pack_chunk(full):
        tail = full[:, 128:256]
        both = tail[0:128] + half_turn(tail[128:256])
        return jnp.concatenate([full[:, 0:128], both], axis=0)

    def unpack_chunk(packed):
        tail = packed[256:384]
        live = lanes_of((128, 128)) < TAIL
        low = jnp.where(live, tail, 0.0)
        high = jnp.where(live, half_turn(tail), 0.0)
        return jnp.concatenate([packed[0:256], jnp.concatenate([low, high], axis=0)], axis=1)

    def chunk2(o):
        return pack_chunk(mm(block_rows(o), wide[...].reshape(2048, 256)))

    ring2 = (up2_s, up2_r, dn2_s, dn2_r, us2, ur2, ds2, dr2)
    agg2 = unpack_chunk(ring_sum(chunk2, own2, *ring2)).astype(bf16).astype(f32)

    logits = sl[...] + agg2
    lanes = lanes_of((256, 256))
    live = lanes < CLASSES

    def tall_of(ref):
        one = jnp.transpose(jnp.broadcast_to(ref[...].astype(f32), (128, 256)))
        return jnp.concatenate([one, one], axis=1)

    hit = lanes.astype(f32) == tall_of(lab)
    train = tall_of(mask)
    log_total = jnp.log(jnp.sum(jnp.where(live, jnp.exp(logits), 0.0), axis=1, keepdims=True))
    cross = log_total - jnp.sum(jnp.where(hit, logits, 0.0), axis=1, keepdims=True)
    prob = jnp.where(live, jnp.exp(logits - log_total), 0.0)
    grad = (train * (prob - hit.astype(f32))).astype(bf16)
    gl[...] = grad
    loss_part = jnp.sum(train[:, 0:1] * cross, axis=0, keepdims=True)
    count_part = jnp.sum(train[:, 0:1], axis=0, keepdims=True)

    def fill(buf, number, parts):
        for b in range(4):
            cut = jnp.concatenate([part[:, b * 128 : (b + 1) * 128] for part in parts], axis=0)
            buf[b * 16 : (b + 1) * 16] = cut.reshape(16, number, 128)

    def to_pair(src, dst, sem, first_s, first_d):
        return pltpu.make_async_remote_copy(
            src_ref=src.at[pl.ds(first_s, 32)], dst_ref=dst.at[pl.ds(first_d, 32)],
            send_sem=sem.at[0], recv_sem=sem.at[1], device_id=(partner, z), device_id_type=MESH,
        )

    def chip_at(dx, k):
        return group_of(dx) * NY + lax.rem(y + k * 3, NY)

    def plane_send(src, dst, sem):
        for dx in range(NX):

            def one(k, c):
                other = chip_at(dx, k)
                pltpu.make_async_remote_copy(
                    src_ref=src.at[other], dst_ref=dst.at[chip], send_sem=sem.at[0], recv_sem=sem.at[1],
                    device_id=(other * 2 + core, z), device_id_type=MESH,
                ).start()
                return c

            lax.fori_loop(1 if dx == 0 else 0, NY, one, 0)

    def plane_gather(buf, sem):
        for dx in range(NX):

            def one(k, c):
                pltpu.make_async_remote_copy(
                    src_ref=buf.at[piece], dst_ref=buf.at[piece], send_sem=sem.at[0], recv_sem=sem.at[1 + dx],
                    device_id=(chip_at(dx, k) * 2 + core, z), device_id_type=MESH,
                ).start()
                return c

            lax.fori_loop(1 if dx == 0 else 0, NY, one, 0)

    def pair_gather(buf, sem, pair_sems):
        copies = []
        for dx in range(NX):
            number = NY - 1 if dx == 0 else NY
            pltpu.make_async_remote_copy(
                src_ref=buf.at[pl.ds(0, number)], dst_ref=buf.at[pl.ds(0, number)],
                send_sem=sem.at[0], recv_sem=sem.at[1 + dx], device_id=(partner, z), device_id_type=MESH,
            ).wait_recv()
            part = pl.ds(core * 32 + from_group(dx) * NY, NY)
            copies.append(pltpu.make_async_remote_copy(
                src_ref=buf.at[part], dst_ref=buf.at[part],
                send_sem=pair_sems.at[dx, 0], recv_sem=pair_sems.at[dx, 1],
                device_id=(partner, z), device_id_type=MESH,
            ))
            copies[-1].start()
        return copies

    def plane_scatter(buf, got, hs, hr, sem):
        hs[...] = (buf[pl.ds(core * 32, 32)] + got[...]).astype(bf16)
        plane_send(hs, hr, sem)
        hr[chip] = hs[chip]

    def col_send(zs, zr, sem):
        def one(k, c):
            pltpu.make_async_remote_copy(
                src_ref=zs, dst_ref=zr.at[z], send_sem=sem.at[0], recv_sem=sem.at[1],
                device_id=(me, lax.rem(z + k, NZ)), device_id_type=MESH,
            ).start()
            return c

        lax.fori_loop(1, NZ, one, 0)
        zr[z] = zs[...]

    def summed(buf):
        return jnp.sum(buf[...].astype(f32), axis=0).astype(bf16)

    piece = core * 32 + chip

    packed = pack_chunk(grad.astype(f32))
    gbuf[z, 0:256] = packed[0:256].astype(bf16)
    gbuf[z, 256:384] = put_scalars(packed[256:384], loss_part, count_part).astype(bf16)

    def pass_on(owner, ssem, rsem, j, h, to):
        part = pl.ds(h * (384 // PARTS), 384 // PARTS)
        return pltpu.make_async_remote_copy(
            src_ref=gbuf.at[owner, part], dst_ref=gbuf.at[owner, part],
            send_sem=ssem.at[j, h], recv_sem=rsem.at[j, h], device_id=(me, to), device_id_type=MESH,
        )

    def up_hop(j, h):
        return pass_on(lax.rem(z + NZ - j, NZ), gus, gur, j, h, above)

    def down_hop(j, h):
        return pass_on(lax.rem(z + j, NZ), gds, gdr, j, h, below)

    def back_chunk(o):
        full = unpack_chunk(gbuf[o].astype(f32))
        return mm(jnp.transpose(full).astype(bf16), block_rows(o))

    for h in range(PARTS):
        up_hop(0, h).start()
        down_hop(0, h).start()
    fill(mine_e, 16, (mm_t(gl[...], hidden[...]),))
    swap_e = to_pair(mine_e, pair_e, pair_e_sem, (1 - core) * 32, 0)
    swap_e.start()
    st[...] = back_chunk(z)

    def both_ways(j, h):
        up_hop(j - 1, h).wait_recv()
        up_hop(j, h).start()
        down_hop(j - 1, h).wait_recv()

        @pl.when(j < DOWN)
        def _():
            down_hop(j, h).start()

    def add_chunks(j):
        st[...] += back_chunk(lax.rem(z + NZ - j, NZ)) + back_chunk(lax.rem(z + j, NZ))

    def gather_step(j, c):
        for h in range(PARTS // 2):
            both_ways(j, h)

        @pl.when(j > 1)
        def _():
            add_chunks(j - 1)

        for h in range(PARTS // 2, PARTS):
            both_ways(j, h)
        return c

    lax.fori_loop(1, 2, gather_step, 0)
    swap_e.wait_recv()
    plane_scatter(mine_e, pair_e, hs_e, hr_e, h_e_sem)
    lax.fori_loop(2, UP, gather_step, 0)
    add_chunks(UP - 1)
    for h in range(PARTS):
        up_hop(UP - 1, h).wait_recv()
    st[...] += back_chunk(lax.rem(z + NZ - UP, NZ))
    col_sums = get_scalars(jnp.sum(gbuf[:, 256:272, :].astype(f32), axis=0))

    for dx in order:
        at = pl.ds(pl.multiple_of(group_of(dx) * 512, 512), 512)
        pack_group(dx, jnp.transpose(st[:, at]), s3, col_sums)
        send_group(dx, s3, r3, a3)
    r3[me] = s3[me]

    all_of(hs_e, hr_e, h_e_sem, 31).wait_recv()
    zs_e[...] = summed(hr_e)
    col_send(zs_e, zr_e, z_e_sem)
    swap_e.wait_send()
    all_of(hs_e, hr_e, h_e_sem, 31).wait_send()
    ring_sent(*ring2)

    def gather_sent(j, c):
        for h in range(PARTS):
            up_hop(j, h).wait_send()

            @pl.when(j < DOWN)
            def _():
                down_hop(j, h).wait_send()

        return c

    lax.fori_loop(0, UP, gather_sent, 0)
    all_of(s2, r2, a2, NR - 1).wait_send()
    all_of(zr_e, zr_e, z_e_sem, NZ - 1).wait_recv()
    fin_e[piece] = summed(zr_e)
    total = jnp.zeros((256, 256), f32)
    for dx in order:
        wait_group(dx, s3, r3, a3)
        if dx == order[-1]:
            plane_gather(fin_e, f_e_sem)
        unpack_group(dx, r3)
        at = pl.ds(pl.multiple_of(from_group(dx) * 512, 512), 512)
        rows_at = wide[pl.ds(from_group(dx) * 16, 16)].reshape(512, 256)
        total = total + mm_t(pick[at, :], rows_at)
    back[...] = total.astype(bf16)
    loss_sum, node_count = get_scalars(jnp.sum(r3[:, 32:48, :].astype(f32), axis=0))

    grad_hidden = mm(gl[...], w2t[0:256]) + mm(back[...], w2t[256:512])
    grad_pre = jnp.where(pre1[...] > 0, grad_hidden, 0.0).astype(bf16)
    parts = (
        mm_t(feat[...], grad_pre),
        mm_t(agg1[...], grad_pre),
        mm_t(back[...], hidden[...]),
    )
    fill(mine, 32, parts)
    swap = to_pair(mine, pair_r, pair_sem, (1 - core) * 32, 0)
    swap.start()
    swap.wait_recv()
    plane_scatter(mine, pair_r, hs, hr, hsem)
    all_of(s3, r3, a3, NR - 1).wait_send()
    swap.wait_send()
    all_of(zr_e, zr_e, z_e_sem, NZ - 1).wait_send()
    swaps_e = pair_gather(fin_e, f_e_sem, pair2_e_sem)
    all_of(hs, hr, hsem, 31).wait_recv()
    zs[...] = summed(hr)
    col_send(zs, zr, zsem)
    all_of(hs, hr, hsem, 31).wait_send()
    all_of(fin_e, fin_e, f_e_sem, 31).wait_send()
    all_of(zr, zr, zsem, NZ - 1).wait_recv()
    fin[piece] = summed(zr)
    plane_gather(fin, fsem)
    for copy in swaps_e:
        copy.wait_recv()
    fin_e_out[...] = fin_e[...]
    all_of(zr, zr, zsem, NZ - 1).wait_send()
    swaps = pair_gather(fin, fsem, pair2_sem)

    lanes = lanes_of((8, 128))
    sums_out[...] = jnp.where(lanes == 0, loss_sum, jnp.where(lanes == 1, node_count, 0.0))
    for copy in swaps:
        copy.wait_recv()
    fin_out[...] = fin[...]
    for copy in swaps + swaps_e:
        copy.wait_send()
    all_of(fin, fin, fsem, 31).wait_send()


def finish(fin, fin_e, sums, g1, g2, g3t, g4t, loss):
    loss_sum, node_count = sums[0:1, 0:1], jnp.maximum(sums[0:1, 1:2], 1.0)
    loss[...] = loss_sum / node_count
    scale = 1.0 / jnp.sqrt(node_count)
    for b in range(4):
        at = slice(b * 128, (b + 1) * 128)
        cut = fin[b * 16 : (b + 1) * 16].astype(f32).reshape(512, 128) * scale
        cut_e = fin_e[b * 16 : (b + 1) * 16].astype(f32).reshape(256, 128) * scale
        g1[:, at] = cut[0:128]
        g2[:, at] = cut[128:256]
        g3t[:, at] = cut_e[0:CLASSES]
        g4t[:, at] = cut[256 : 256 + CLASSES]


def shards(
    features, send_rows, send_count, tile_values, tile_dst, tile_src, tile_count,
    labels, train_mask, w_self1, w_neigh1, w_self2, w_neigh2,
):
    slots = jnp.arange(64, dtype=i32)
    where = tile_dst.reshape(1, 64) * 16 + tile_src.reshape(1, 64)
    here = (jnp.arange(384, dtype=i32)[:, None] == where) & (slots < tile_count.reshape(()))[None, :]
    cell = jnp.min(jnp.where(here, slots[None, :], 64), axis=1)
    vm = pl.BlockSpec(memory_space=pltpu.VMEM)
    sm = pl.BlockSpec(memory_space=pltpu.SMEM)
    V = pltpu.VMEM
    dma = pltpu.SemaphoreType.DMA
    fin, fin_e, sums = pl.pallas_call(
        kernel,
        out_shape=[
            jax.ShapeDtypeStruct((64, 32, 128), bf16),
            jax.ShapeDtypeStruct((64, 16, 128), bf16),
            jax.ShapeDtypeStruct((8, 128), f32),
        ],
        in_specs=[sm, vm, vm, vm, pl.BlockSpec(memory_space=pl.ANY), vm, vm, vm, vm, vm, vm],
        out_specs=[vm] * 3,
        scratch_shapes=[
            V((512, 512), bf16),
            V((65, 128, 128), bf16),
            V((3072, 2048), bf16),
            V((2048, 256), bf16),
            V((64, 32, 128), bf16), V((64, 32, 128), bf16),
            V((64, 48, 128), bf16), V((64, 48, 128), bf16),
            V((64, 48, 128), bf16), V((64, 48, 128), bf16),
            V((64, 32, 256), bf16),
            V((UP, 256, 128), f32), V((UP + 1, 256, 128), f32),
            V((DOWN, 256, 128), f32), V((DOWN + 1, 256, 128), f32),
            V((UP, 384, 128), bf16), V((UP + 1, 384, 128), bf16),
            V((DOWN, 384, 128), bf16), V((DOWN + 1, 384, 128), bf16),
            V((NZ, 384, 128), bf16),
            V((256, 2048), f32),
            V((2, 2, 256, 128), f32), V((2, 2, 384, 128), f32),
            V((256, 512), f32),
            V((256, 512), bf16),
            V((256, 128), bf16),
            V((256, 256), bf16),
            V((256, 256), f32),
            V((256, 256), bf16),
            V((256, 256), bf16),
            V((64, 32, 128), f32), V((32, 32, 128), f32),
            V((32, 32, 128), bf16), V((32, 32, 128), bf16),
            V((32, 128), bf16), V((NZ, 32, 128), bf16),
            V((64, 32, 128), bf16),
            V((64, 16, 128), f32), V((32, 16, 128), f32),
            V((32, 16, 128), bf16), V((32, 16, 128), bf16),
            V((16, 128), bf16), V((NZ, 16, 128), bf16),
            V((64, 16, 128), bf16),
            dma, dma((1 + NX,)), dma((1 + NX,)), dma((1 + NX,)),
            dma((UP, PARTS)), dma((UP, PARTS)), dma((DOWN, PARTS)), dma((DOWN, PARTS)),
            dma((UP, PARTS)), dma((UP, PARTS)), dma((DOWN, PARTS)), dma((DOWN, PARTS)),
            dma((UP, PARTS)), dma((UP, PARTS)), dma((DOWN, PARTS)), dma((DOWN, PARTS)),
            dma((2,)), dma((2,)), dma((2,)), dma((1 + NX,)), dma((NX, 2)),
            dma((2,)), dma((2,)), dma((2,)), dma((1 + NX,)), dma((NX, 2)),
        ],
        compiler_params=pltpu.CompilerParams(
            collective_id=0, has_side_effects=True, vmem_limit_bytes=56 * 1024 * 1024
        ),
        name="sage_step",
    )(
        cell, features, send_rows.reshape(1, 2048), send_count.reshape(1, 64),
        tile_values.reshape(64, 128, 128), labels.reshape(1, 256), train_mask.reshape(1, 256),
        w_self1, w_neigh1, w_self2.T, w_neigh2.T,
    )
    g1, g2, g3t, g4t, loss = pl.pallas_call(
        finish,
        out_shape=[
            jax.ShapeDtypeStruct((128, 512), f32),
            jax.ShapeDtypeStruct((128, 512), f32),
            jax.ShapeDtypeStruct((CLASSES, 512), f32),
            jax.ShapeDtypeStruct((CLASSES, 512), f32),
            jax.ShapeDtypeStruct((1, 1), f32),
        ],
        in_specs=[vm] * 3,
        out_specs=[vm] * 5,
        compiler_params=pltpu.CompilerParams(vmem_limit_bytes=56 * 1024 * 1024),
        name="sage_finish",
    )(fin, fin_e, sums)
    return g1, g2, g3t.T, g4t.T, loss.reshape(())


def solution(mesh):
    in_specs = (
        P(("row", "col"), None),
        P("row", "col", None),
        P("row", "col", None),
        P("row", "col", None, None, None),
        P("row", "col", None),
        P("row", "col", None),
        P("row", "col"),
        P(("row", "col")),
        P(("row", "col")),
        P(),
        P(),
        P(),
        P(),
    )
    out_specs = (P(), P(), P(), P(), P())
    return jax.shard_map(shards, mesh=mesh, in_specs=in_specs, out_specs=out_specs, check_vma=False)
```
